512 devices in a mesh: dp: 32 (over y_lo, z), tensor: 16 (over x, y_hi, core).
Axes of the slice: x: 4, y: 8 (y_hi: 2, y_lo: 4; y = y_hi * 4 + y_lo), z: 8, core: 2. Of those that a mesh axis runs over, the one named last changes fastest.
Arguments:
- tokens: bfloat16 [4096, 4096], P(('dp', 'tensor')), may hold values from -6 to 6
- upstream_grad: bfloat16 [4096, 4096], P(('dp', 'tensor')), may hold values from -24 to 24
- w_gate: bfloat16 [4096, 14336], P(None, 'tensor'), may hold values from -0.09375 to 0.09375
- w_up: bfloat16 [4096, 14336], P(None, 'tensor'), may hold values from -0.09375 to 0.09375
- w_down: bfloat16 [14336, 4096], P('tensor'), may hold values from -0.046875 to 0.046875
Outputs:
- grad_tokens: bfloat16 [4096, 4096], P(('dp', 'tensor'))
- grad_down: float32 [14336, 4096], P('tensor', 'dp')
The draws below stay inside these ranges and needn't reach their ends.
All inputs are finite; a program needn't handle non-finite values.
Results may differ from the reference program's by a relative error of at most 0.03.
Values may be sent and summed in bfloat16 or wider, within the bound.
No kernel may reach another device: no remote copies, remote signals or barrier semaphores. Data moves between devices by JAX's collectives and lax.ppermute only.
A program may use at most 128 MiB of HBM per device.

```python
import jax
import jax.numpy as jnp
from jax import lax

D = 4096
F_DEV = 896
FF = 14336
TOKENS = 4096
N_TENSOR = 16


def spiked(values, rng, source, target, shards_of, factor):
    owner, partner = [(jnp.arange(values.shape[position]) // (values.shape[position] // shards_of)).reshape([-1 if axis == position else 1 for axis in range(values.ndim)]) for position in (source, target)]
    chosen = jax.random.permutation(rng, shards_of)[partner]
    strong = (owner == chosen) | (owner == (partner + shards_of // 2) % shards_of)
    return jnp.where(strong, factor * values, values)


def shard_levels(rng, extent, pieces, low, high):
    def one(axis_at, shards_of):
        draws = jax.random.uniform(jax.random.fold_in(jax.random.fold_in(rng, 6), axis_at), (shards_of,), jnp.float32, low / len(pieces), high / len(pieces))
        return jnp.repeat(jnp.exp(draws), extent[axis_at] // shards_of).reshape((-1,) + (1,) * (len(extent) - axis_at - 1))

    level = one(*pieces[0])
    for cut in pieces[1:]:
        level = level * one(*cut)
    return level


def normal_values(own_key, shape, width, reach, pieces=(), kind=jnp.bfloat16):
    values = width * jax.random.normal(own_key, shape, jnp.float32)
    if pieces:
        values = values * shard_levels(own_key, shape, pieces, -0.22, 0.18)
    return jnp.clip(values, -reach, reach).astype(kind)


def noise_with(rng, dims, deviation, limit, split, heavy, kind=jnp.bfloat16):
    array = deviation * jax.random.normal(rng, dims, jnp.float32)
    if split:
        array = array * shard_levels(rng, dims, split, -0.22, 0.18)
    return jnp.clip(spiked(array, jax.random.fold_in(rng, 3), *heavy), -limit, limit).astype(kind)


def setup_inputs(seed: int = 0) -> dict:
    seeds = jax.random.split(jax.random.key(seed), 6)
    tokens = normal_values(seeds[0], (TOKENS, D), 1.0, 6.0, ((0, 512),))
    upstream_grad = noise_with(seeds[1], (TOKENS, D), 1.0, 24.0, ((0, 512),), (0, 1, 512, 6.0))
    w_gate = normal_values(seeds[2], (D, FF), D ** -0.5, 0.09375, ((1, 16),))
    w_up = normal_values(seeds[3], (D, FF), D ** -0.5, 0.09375, ((1, 16),))
    w_down = normal_values(seeds[4], (FF, D), FF ** -0.5, 0.046875, ((0, 16),))
    return dict(tokens=tokens, upstream_grad=upstream_grad, w_gate=w_gate, w_up=w_up, w_down=w_down)


def reference(tokens, upstream_grad, w_gate, w_up, w_down):
    gate_pre = jnp.dot(tokens, w_gate, preferred_element_type=jnp.float32)
    up_pre = jnp.dot(tokens, w_up, preferred_element_type=jnp.float32)
    sig_gate = jax.nn.sigmoid(gate_pre)
    act_gate = gate_pre * sig_gate
    hidden = (act_gate * up_pre).astype(jnp.bfloat16)
    grad_hidden = jnp.dot(upstream_grad, w_down.T, preferred_element_type=jnp.float32).astype(jnp.bfloat16)
    hidden_f = grad_hidden.astype(jnp.float32)
    grad_gate = (hidden_f * up_pre * sig_gate * (1.0 + gate_pre * (1.0 - sig_gate))).astype(jnp.bfloat16)
    grad_up = (hidden_f * act_gate).astype(jnp.bfloat16)

    def add_block(running, block_index):
        first = (block_index * F_DEV).astype(jnp.int32)
        gate_blk = lax.dynamic_slice_in_dim(grad_gate, first, F_DEV, 1)
        up_blk = lax.dynamic_slice_in_dim(grad_up, first, F_DEV, 1)
        wgate_blk = lax.dynamic_slice_in_dim(w_gate, first, F_DEV, 1)
        wup_blk = lax.dynamic_slice_in_dim(w_up, first, F_DEV, 1)
        term = jnp.dot(gate_blk, wgate_blk.T, preferred_element_type=jnp.float32)
        term = term + jnp.dot(up_blk, wup_blk.T, preferred_element_type=jnp.float32)
        rounded = lax.optimization_barrier(term.astype(jnp.bfloat16))
        return running + rounded.astype(jnp.float32), None

    start_sum = jnp.zeros((TOKENS, D), jnp.float32)
    total, unused = lax.scan(add_block, start_sum, jnp.arange(N_TENSOR, dtype=jnp.int32))
    grad_tokens = total.astype(jnp.bfloat16)
    factor = float(TOKENS) ** -0.5
    grad_down = jnp.dot(hidden.T, upstream_grad, preferred_element_type=jnp.float32) * factor
    return grad_tokens, grad_down
```

```python
import jax
import jax.numpy as jnp
from jax import lax
from jax.sharding import Mesh, PartitionSpec as P

SIZES = (4, 8, 4, 2, 2)
NAMES = ("ylo", "z", "x", "yhi", "core")
SWAP = [(0, 1), (1, 0)]


def contract_rows(left, right):
    return lax.dot_general(
        left, right, (((0,), (0,)), ((), ())), preferred_element_type=jnp.float32
    )


def contract_cols(left, right):
    return lax.dot_general(
        left, right, (((1,), (1,)), ((), ())), preferred_element_type=jnp.float32
    )


def swap(value, axis):
    return lax.ppermute(value, axis, SWAP)


def both(rows, axis):
    return jnp.concatenate([rows, swap(rows, axis)], axis=0)


def gather_a2a(rows, axis):
    n = lax.axis_size(axis)
    copies = jnp.broadcast_to(rows[None], (n,) + rows.shape)
    return lax.all_to_all(copies, axis, 0, 0).reshape((n * rows.shape[0],) + rows.shape[1:])


def after(value, *earlier):
    return lax.optimization_barrier((value,) + earlier)[0]


def body(tokens, upstream_grad, w_gate, w_up, w_down):
    rows, width = tokens.shape
    f_dev = w_gate.shape[1]
    n_y, n_z, n_x = lax.axis_size("ylo"), lax.axis_size("z"), lax.axis_size("x")
    block = width // (n_y * n_z)

    tokens2 = both(tokens, "yhi")
    upstream2 = both(upstream_grad, "yhi")
    cols = upstream_grad.reshape(rows, n_y, n_z, block).transpose(2, 0, 1, 3)
    cols = cols.reshape(n_z * rows, n_y * block)
    cols = lax.all_to_all(cols, "z", 0, 0, tiled=True)
    cols2 = both(cols, "yhi")

    tokens_x = lax.all_gather(tokens2, "x", axis=0, tiled=True)
    upstream_x = gather_a2a(after(upstream2, tokens_x), "x")
    gathered = both(tokens_x, "core")
    gate_pre = jnp.dot(gathered, w_gate, preferred_element_type=jnp.float32)
    up_pre = jnp.dot(gathered, w_up, preferred_element_type=jnp.float32)
    sig_gate = jax.nn.sigmoid(gate_pre)
    act_gate = gate_pre * sig_gate
    hidden = (act_gate * up_pre).astype(jnp.bfloat16)
    hidden_z = gather_a2a(after(hidden, upstream_x), "z")

    upstream = both(after(upstream_x, hidden), "core")
    grad_hidden = contract_cols(upstream, w_down).astype(jnp.bfloat16)
    hidden_f = grad_hidden.astype(jnp.float32)
    grad_gate = (hidden_f * up_pre * sig_gate * (1.0 + gate_pre * (1.0 - sig_gate))).astype(
        jnp.bfloat16
    )
    grad_up = (hidden_f * act_gate).astype(jnp.bfloat16)
    partial = (contract_cols(grad_gate, w_gate) + contract_cols(grad_up, w_up)).astype(jnp.bfloat16)

    half = partial.shape[0] // 2
    other = swap(partial[half:], "core")
    partial = (partial[:half].astype(jnp.float32) + other.astype(jnp.float32)).astype(jnp.bfloat16)

    cols = both(lax.all_gather(after(cols2, hidden), "x", axis=0, tiled=True), "core")
    n_t = cols.shape[0] // (n_z * rows)
    cols = cols.reshape(n_t, n_z, rows, n_y * block).transpose(1, 0, 2, 3)
    cols = cols.reshape(n_z * n_t * rows, n_y * block)
    factor = float(n_z * n_t * rows * n_y) ** (-0.5)
    parts = [
        (contract_rows(hidden_z, cols[:, i * block : (i + 1) * block]) * factor).astype(jnp.bfloat16)
        for i in range(n_y)
    ]
    down = lax.all_to_all(jnp.concatenate(parts, axis=0), "ylo", 0, 0, tiled=True)

    me = lax.axis_index("x")
    chunk = 2 * rows
    total = lax.dynamic_slice_in_dim(partial, me * chunk, chunk, 0).astype(jnp.float32)
    for k in range(1, n_x):
        piece = lax.dynamic_slice_in_dim(partial, lax.rem(me + k, n_x) * chunk, chunk, 0)
        piece = lax.ppermute(piece, "x", [(i, (i + k) % n_x) for i in range(n_x)])
        total = total + piece.astype(jnp.float32)
    other = swap(total[rows:].astype(jnp.bfloat16), "yhi")
    summed = (total[:rows] + other.astype(jnp.float32)).astype(jnp.bfloat16)

    grad_down = down.reshape(n_y, f_dev, block).astype(jnp.float32).sum(0)
    return (summed, grad_down)


def solution(mesh):
    cut = Mesh(mesh.devices.reshape(SIZES), NAMES)
    dp, tensor = NAMES[:2], NAMES[2:]
    in_specs = (
        P(dp + tensor, None),
        P(dp + tensor, None),
        P(None, tensor),
        P(None, tensor),
        P(tensor, None),
    )
    out_specs = (P(dp + tensor, None), P(tensor, dp))
    return jax.shard_map(body, mesh=cut, in_specs=in_specs, out_specs=out_specs, check_vma=False)
```

```python
import jax
import jax.numpy as jnp
from jax import lax
from jax.sharding import Mesh, PartitionSpec as P

SIZES = (4, 8, 4, 2, 2)
NAMES = ("ylo", "z", "x", "yhi", "core")
SWAP = [(0, 1), (1, 0)]


def contract_rows(left, right):
    return lax.dot_general(
        left, right, (((0,), (0,)), ((), ())), preferred_element_type=jnp.float32
    )


def contract_cols(left, right):
    return lax.dot_general(
        left, right, (((1,), (1,)), ((), ())), preferred_element_type=jnp.float32
    )


def swap(value, axis):
    return lax.ppermute(value, axis, SWAP)


def both(rows, axis):
    return jnp.concatenate([rows, swap(rows, axis)], axis=0)


def gather_a2a(value, axis):
    copies = jnp.broadcast_to(value, (lax.axis_size(axis),) + value.shape[1:])
    return lax.all_to_all(copies, axis, 0, 0)


def after(value, *earlier):
    return lax.optimization_barrier((value,) + earlier)[0]


def in_order(own, other, index):
    first, second = jnp.where(index == 0, own, other), jnp.where(index == 0, other, own)
    return jnp.concatenate([first, second], axis=0)


def body(tokens, upstream_grad, w_gate, w_up, w_down):
    rows, width = tokens.shape
    f_dev = w_gate.shape[1]
    n_y, n_z, n_x = lax.axis_size("ylo"), lax.axis_size("z"), lax.axis_size("x")
    block = width // (n_y * n_z)

    cols = upstream_grad.reshape(rows, n_y, n_z * block).transpose(1, 0, 2)
    me_h = lax.axis_index("yhi")
    cols = jnp.broadcast_to(cols[:, None], (n_y, 2, rows, n_z * block))
    cols = lax.all_to_all(cols.reshape(2 * n_y, rows, -1), ("ylo", "yhi"), 0, 0)
    cols = cols.reshape(n_y, 2, rows, n_z * block).transpose(1, 2, 0, 3).reshape(2 * rows, width)

    other = swap(jnp.concatenate([tokens, upstream_grad], axis=0), "yhi")
    tokens2 = in_order(tokens, other[:rows], me_h)
    upstream2 = in_order(upstream_grad, other[rows:], me_h)
    pair = jnp.stack([upstream2, cols], axis=0)[None]

    tokens_x = lax.all_gather(tokens2, "x", axis=0, tiled=True)
    gathered = both(tokens_x, "core")
    pair_x = gather_a2a(after(pair, tokens_x), "x")
    gate_pre = jnp.dot(gathered, w_gate, preferred_element_type=jnp.float32)
    up_pre = jnp.dot(gathered, w_up, preferred_element_type=jnp.float32)
    sig_gate = jax.nn.sigmoid(gate_pre)
    act_gate = gate_pre * sig_gate
    hidden = (act_gate * up_pre).astype(jnp.bfloat16)

    hidden_y = lax.all_gather(hidden, "ylo", axis=0)
    pair_x = after(pair_x, hidden_y)
    cols = both(pair_x[:, 1].reshape(-1, width), "core").reshape(-1, n_y, n_z * block)
    factor = float(n_z * cols.shape[0] * n_y) ** (-0.5)
    down = lax.dot_general(
        hidden_y, cols, (((0, 1), (1, 0)), ((), ())), preferred_element_type=jnp.float32
    )
    down = (down * factor).astype(jnp.bfloat16).reshape(f_dev, n_z, block).transpose(1, 0, 2)
    down_z = lax.all_to_all(down, "z", 0, 0)

    upstream = both(after(pair_x, down)[:, 0].reshape(-1, width), "core")
    grad_hidden = contract_cols(upstream, w_down).astype(jnp.bfloat16)
    hidden_f = grad_hidden.astype(jnp.float32)
    grad_gate = (hidden_f * up_pre * sig_gate * (1.0 + gate_pre * (1.0 - sig_gate))).astype(
        jnp.bfloat16
    )
    grad_up = (hidden_f * act_gate).astype(jnp.bfloat16)
    partial = (contract_cols(grad_gate, w_gate) + contract_cols(grad_up, w_up)).astype(jnp.bfloat16)

    half = partial.shape[0] // 2
    other = []
    for k in range(2):
        cut = partial[half:, k * width // 2 : (k + 1) * width // 2]
        cut = lax.all_gather(cut, "core", axis=0)
        other.append(lax.dynamic_index_in_dim(cut, 1 - lax.axis_index("core"), 0, keepdims=False))
    other = jnp.concatenate(other, axis=1)
    partial = (partial[:half].astype(jnp.float32) + other.astype(jnp.float32)).astype(jnp.bfloat16)
    me = lax.axis_index("x")
    chunk = 2 * rows
    total = lax.dynamic_slice_in_dim(partial, me * chunk, chunk, 0).astype(jnp.float32)
    for k in range(1, n_x):
        piece = lax.dynamic_slice_in_dim(partial, lax.rem(me + k, n_x) * chunk, chunk, 0)
        piece = lax.ppermute(piece, "x", [(i, (i + k) % n_x) for i in range(n_x)])
        total = total + piece.astype(jnp.float32)
    total = total.reshape(2, rows, width)
    mine = lax.dynamic_index_in_dim(total, me_h, 0, keepdims=False)
    sent = lax.dynamic_index_in_dim(total, 1 - me_h, 0, keepdims=False).astype(jnp.bfloat16)
    sent = lax.all_gather(sent, "yhi", axis=0)
    other = lax.dynamic_index_in_dim(sent, 1 - me_h, 0, keepdims=False)
    summed = (mine + other.astype(jnp.float32)).astype(jnp.bfloat16)

    grad_down = down_z.astype(jnp.float32).sum(0)
    return (summed, grad_down)


def solution(mesh):
    cut = Mesh(mesh.devices.reshape(SIZES), NAMES)
    dp, tensor = NAMES[:2], NAMES[2:]
    in_specs = (
        P(dp + tensor, None),
        P(dp + tensor, None),
        P(None, tensor),
        P(None, tensor),
        P(tensor, None),
    )
    out_specs = (P(dp + tensor, None), P(tensor, dp))
    return jax.shard_map(body, mesh=cut, in_specs=in_specs, out_specs=out_specs, check_vma=False)
```

```python
import jax
import jax.numpy as jnp
from jax import lax
from jax.sharding import Mesh, PartitionSpec as P

SIZES = (4, 8, 4, 2, 2)
NAMES = ("ylo", "z", "x", "yhi", "core")
SWAP = [(0, 1), (1, 0)]


def contract_rows(left, right):
    return lax.dot_general(
        left, right, (((0,), (0,)), ((), ())), preferred_element_type=jnp.float32
    )


def contract_cols(left, right):
    return lax.dot_general(
        left, right, (((1,), (1,)), ((), ())), preferred_element_type=jnp.float32
    )


def swap(value, axis):
    return lax.ppermute(value, axis, SWAP)


def both(rows, axis):
    return jnp.concatenate([rows, swap(rows, axis)], axis=0)


def gather_a2a(value, axis):
    copies = jnp.broadcast_to(value, (lax.axis_size(axis),) + value.shape[1:])
    return lax.all_to_all(copies, axis, 0, 0)


def after(value, *earlier):
    return lax.optimization_barrier((value,) + earlier)[0]


def in_order(own, other, index):
    first, second = jnp.where(index == 0, own, other), jnp.where(index == 0, other, own)
    return jnp.concatenate([first, second], axis=0)


def body(tokens, upstream_grad, w_gate, w_up, w_down):
    rows, width = tokens.shape
    f_dev = w_gate.shape[1]
    n_y, n_z, n_x = lax.axis_size("ylo"), lax.axis_size("z"), lax.axis_size("x")
    block = width // (n_y * n_z)

    me_h = lax.axis_index("yhi")
    cols = upstream_grad.reshape(rows, n_y, n_z * block).transpose(1, 0, 2)
    cols = jnp.broadcast_to(cols[:, None], (n_y, 4, rows, n_z * block))
    cols = lax.all_to_all(cols.reshape(4 * n_y, rows, -1), ("ylo", "yhi", "core"), 0, 0)
    cols = cols.reshape(n_y, 2, 2, rows, n_z * block).transpose(2, 1, 3, 0, 4)
    cols = cols.reshape(2, 2 * rows, width)
    cols = in_order(cols[0], cols[1], lax.axis_index("core"))

    other = swap(jnp.concatenate([tokens, upstream_grad], axis=0), "yhi")
    tokens2 = in_order(tokens, other[:rows], me_h)
    upstream2 = in_order(upstream_grad, other[rows:], me_h)
    pair = jnp.concatenate([upstream2, cols], axis=0).reshape(1, 3, 2 * rows, width)

    tokens_x = lax.all_gather(tokens2, "x", axis=0, tiled=True)
    gathered = both(tokens_x, "core")
    pair_x = gather_a2a(after(pair, tokens_x), "x")
    gate_pre = jnp.dot(gathered, w_gate, preferred_element_type=jnp.float32)
    up_pre = jnp.dot(gathered, w_up, preferred_element_type=jnp.float32)
    sig_gate = jax.nn.sigmoid(gate_pre)
    act_gate = gate_pre * sig_gate
    hidden = (act_gate * up_pre).astype(jnp.bfloat16)

    hidden_y = lax.all_gather(hidden, "ylo", axis=0)
    pair_x = after(pair_x, hidden_y)
    cols = pair_x[:, 1:].transpose(1, 0, 2, 3).reshape(-1, n_y, n_z * block)
    factor = float(n_z * cols.shape[0] * n_y) ** (-0.5)
    down = lax.dot_general(
        hidden_y, cols, (((0, 1), (1, 0)), ((), ())), preferred_element_type=jnp.float32
    )
    down = (down * factor).astype(jnp.bfloat16).reshape(f_dev, n_z, block).transpose(1, 0, 2)
    down_z = lax.all_to_all(down, "z", 0, 0)

    upstream = both(after(pair_x[:, 0].reshape(-1, width), down), "core")
    grad_hidden = contract_cols(upstream, w_down).astype(jnp.bfloat16)
    hidden_f = grad_hidden.astype(jnp.float32)
    grad_gate = (hidden_f * up_pre * sig_gate * (1.0 + gate_pre * (1.0 - sig_gate))).astype(
        jnp.bfloat16
    )
    grad_up = (hidden_f * act_gate).astype(jnp.bfloat16)
    partial = (contract_cols(grad_gate, w_gate) + contract_cols(grad_up, w_up)).astype(jnp.bfloat16)

    half = partial.shape[0] // 2
    other = []
    for k in range(2):
        cut = partial[half:, k * width // 2 : (k + 1) * width // 2]
        cut = lax.all_gather(cut, "core", axis=0)
        other.append(lax.dynamic_index_in_dim(cut, 1 - lax.axis_index("core"), 0, keepdims=False))
    other = jnp.concatenate(other, axis=1)
    partial = (partial[:half].astype(jnp.float32) + other.astype(jnp.float32)).astype(jnp.bfloat16)
    me = lax.axis_index("x")
    chunk = 2 * rows
    total = lax.dynamic_slice_in_dim(partial, me * chunk, chunk, 0).astype(jnp.float32)
    for k in range(1, n_x):
        piece = lax.dynamic_slice_in_dim(partial, lax.rem(me + k, n_x) * chunk, chunk, 0)
        piece = lax.ppermute(piece, "x", [(i, (i + k) % n_x) for i in range(n_x)])
        total = total + piece.astype(jnp.float32)
    total = total.reshape(2, rows, width)
    mine = lax.dynamic_index_in_dim(total, me_h, 0, keepdims=False)
    sent = lax.dynamic_index_in_dim(total, 1 - me_h, 0, keepdims=False).astype(jnp.bfloat16)
    sent = lax.all_gather(sent, "yhi", axis=0)
    other = lax.dynamic_index_in_dim(sent, 1 - me_h, 0, keepdims=False)
    summed = (mine + other.astype(jnp.float32)).astype(jnp.bfloat16)

    grad_down = down_z.astype(jnp.float32).sum(0)
    return (summed, grad_down)


def solution(mesh):
    cut = Mesh(mesh.devices.reshape(SIZES), NAMES)
    dp, tensor = NAMES[:2], NAMES[2:]
    in_specs = (
        P(dp + tensor, None),
        P(dp + tensor, None),
        P(None, tensor),
        P(None, tensor),
        P(tensor, None),
    )
    out_specs = (P(dp + tensor, None), P(tensor, dp))
    return jax.shard_map(body, mesh=cut, in_specs=in_specs, out_specs=out_specs, check_vma=False)
```

```python
import jax
import jax.numpy as jnp
from jax import lax
from jax.sharding import Mesh, PartitionSpec as P

SIZES = (4, 8, 4, 2, 2)
NAMES = ("ylo", "z", "x", "yhi", "core")
SWAP = [(0, 1), (1, 0)]


def contract_rows(left, right):
    return lax.dot_general(
        left, right, (((0,), (0,)), ((), ())), preferred_element_type=jnp.float32
    )


def contract_cols(left, right):
    return lax.dot_general(
        left, right, (((1,), (1,)), ((), ())), preferred_element_type=jnp.float32
    )


def swap(value, axis):
    return lax.ppermute(value, axis, SWAP)


def both(rows, axis):
    return jnp.concatenate([rows, swap(rows, axis)], axis=0)


def gather_a2a(value, axis):
    copies = jnp.broadcast_to(value, (lax.axis_size(axis),) + value.shape[1:])
    return lax.all_to_all(copies, axis, 0, 0)


def after(value, *earlier):
    return lax.optimization_barrier((value,) + earlier)[0]


def in_order(own, other, index):
    first, second = jnp.where(index == 0, own, other), jnp.where(index == 0, other, own)
    return jnp.concatenate([first, second], axis=0)


def body(tokens, upstream_grad, w_gate, w_up, w_down):
    rows, width = tokens.shape
    f_dev = w_gate.shape[1]
    n_y, n_z, n_x = lax.axis_size("ylo"), lax.axis_size("z"), lax.axis_size("x")
    block = width // (n_y * n_z)

    me_h = lax.axis_index("yhi")
    cols = upstream_grad.reshape(rows, n_y, n_z * block).transpose(1, 0, 2)
    cols = jnp.broadcast_to(cols[:, None], (n_y, 4, rows, n_z * block))
    cols = lax.all_to_all(cols.reshape(4 * n_y, rows, -1), ("ylo", "yhi", "core"), 0, 0)
    cols = cols.reshape(n_y, 2, 2, rows, n_z * block).transpose(2, 1, 3, 0, 4)
    cols = cols.reshape(2, 2 * rows, width)
    cols = in_order(cols[0], cols[1], lax.axis_index("core"))

    other = swap(jnp.concatenate([tokens, upstream_grad], axis=0), "yhi")
    tokens2 = in_order(tokens, other[:rows], me_h)
    upstream2 = in_order(upstream_grad, other[rows:], me_h)
    pair = jnp.concatenate([upstream2, cols], axis=0).reshape(1, 3, 2 * rows, width)

    tokens_x = lax.all_gather(tokens2, "x", axis=0, tiled=True)
    gathered = tokens_x.reshape(n_x, 1, 2 * rows, width)
    gathered = jnp.concatenate([gathered, swap(gathered, "core")], axis=1).reshape(-1, width)
    pair_x = gather_a2a(after(pair, tokens_x), "x")
    gate_pre = jnp.dot(gathered, w_gate, preferred_element_type=jnp.float32)
    up_pre = jnp.dot(gathered, w_up, preferred_element_type=jnp.float32)
    sig_gate = jax.nn.sigmoid(gate_pre)
    act_gate = gate_pre * sig_gate
    hidden = (act_gate * up_pre).astype(jnp.bfloat16)

    hidden_y = lax.all_gather(hidden, "ylo", axis=0)
    pair_x = after(pair_x, hidden_y)
    cols = pair_x[:, 1:].reshape(-1, n_y, n_z * block)
    factor = float(n_z * cols.shape[0] * n_y) ** (-0.5)
    down = lax.dot_general(
        hidden_y, cols, (((0, 1), (1, 0)), ((), ())), preferred_element_type=jnp.float32
    )
    down = (down * factor).astype(jnp.bfloat16).reshape(f_dev, n_z, block).transpose(1, 0, 2)
    down_z = lax.all_to_all(down, "z", 0, 0)

    upstream = after(pair_x[:, :1], down)
    upstream = jnp.concatenate([upstream, swap(upstream, "core")], axis=1).reshape(-1, width)
    grad_hidden = contract_cols(upstream, w_down).astype(jnp.bfloat16)
    hidden_f = grad_hidden.astype(jnp.float32)
    grad_gate = (hidden_f * up_pre * sig_gate * (1.0 + gate_pre * (1.0 - sig_gate))).astype(
        jnp.bfloat16
    )
    grad_up = (hidden_f * act_gate).astype(jnp.bfloat16)
    partial = (contract_cols(grad_gate, w_gate) + contract_cols(grad_up, w_up)).astype(jnp.bfloat16)

    partial = partial.reshape(n_x, 2, 2 * rows, width)
    away, partial = (partial[:, k].reshape(-1, width) for k in (1, 0))
    other = []
    for k in range(2):
        cut = away[:, k * width // 2 : (k + 1) * width // 2]
        cut = lax.all_gather(cut, "core", axis=0)
        other.append(lax.dynamic_index_in_dim(cut, 1 - lax.axis_index("core"), 0, keepdims=False))
    other = jnp.concatenate(other, axis=1)
    partial = (partial.astype(jnp.float32) + other.astype(jnp.float32)).astype(jnp.bfloat16)
    me = lax.axis_index("x")
    chunk = 2 * rows
    total = lax.dynamic_slice_in_dim(partial, me * chunk, chunk, 0).astype(jnp.float32)
    for k in range(1, n_x):
        piece = lax.dynamic_slice_in_dim(partial, lax.rem(me + k, n_x) * chunk, chunk, 0)
        piece = lax.ppermute(piece, "x", [(i, (i + k) % n_x) for i in range(n_x)])
        total = total + piece.astype(jnp.float32)
    total = total.reshape(2, rows, width)
    mine = lax.dynamic_index_in_dim(total, me_h, 0, keepdims=False)
    sent = lax.dynamic_index_in_dim(total, 1 - me_h, 0, keepdims=False).astype(jnp.bfloat16)
    sent = lax.all_gather(sent, "yhi", axis=0)
    other = lax.dynamic_index_in_dim(sent, 1 - me_h, 0, keepdims=False)
    summed = (mine + other.astype(jnp.float32)).astype(jnp.bfloat16)

    grad_down = down_z.astype(jnp.float32).sum(0)
    return (summed, grad_down)


def solution(mesh):
    cut = Mesh(mesh.devices.reshape(SIZES), NAMES)
    dp, tensor = NAMES[:2], NAMES[2:]
    in_specs = (
        P(dp + tensor, None),
        P(dp + tensor, None),
        P(None, tensor),
        P(None, tensor),
        P(tensor, None),
    )
    out_specs = (P(dp + tensor, None), P(tensor, dp))
    return jax.shard_map(body, mesh=cut, in_specs=in_specs, out_specs=out_specs, check_vma=False)
```
